32 devices in a mesh: section: 2 (over x), fsdp: 4 (over y, core), rep: 4 (over z).
Axes of the slice: x: 2, y: 2, z: 4, core: 2. Of those that a mesh axis runs over, the one named last changes fastest.
Arguments:
- inputs: bfloat16 [2, 16, 640, 768], P(None, ('fsdp', 'rep')), may hold values from -6 to 6
- cotangent: bfloat16 [2, 16, 640, 768], P(None, ('fsdp', 'rep')), may hold values from -6 to 6
- live_slots: int32 [2, 16], P(None, ('fsdp', 'rep')), may hold values from 0 to 1, as said below
- gain_one: bfloat16 [2, 768], P('section', 'fsdp'), may hold values from 0.5 to 1.5
- shift_one: bfloat16 [2, 768], P('section', 'fsdp'), may hold values from -2 to 2
- project: bfloat16 [2, 768, 2304], P('section', 'fsdp'), may hold values from -0.21875 to 0.21875
- bias_query: bfloat16 [2, 768], P('section', 'fsdp'), may hold values from -3 to 3
- bias_value: bfloat16 [2, 768], P('section', 'fsdp'), may hold values from -2 to 2
- output: bfloat16 [2, 768, 768], P('section', 'fsdp'), may hold values from -3.5 to 3.5
- bias_output: bfloat16 [2, 768], P('section', 'fsdp'), may hold values from -2 to 2
- gain_two: bfloat16 [2, 768], P('section', 'fsdp'), may hold values from 0.5 to 1.5
- shift_two: bfloat16 [2, 768], P('section', 'fsdp'), may hold values from -2 to 2
- expand: bfloat16 [2, 768, 3072], P('section', 'fsdp'), may hold values from -0.21875 to 0.21875
- bias_expand: bfloat16 [2, 3072], P('section', 'fsdp'), may hold values from -3 to 3
- contract: bfloat16 [2, 3072, 768], P('section', 'fsdp'), may hold values from -0.15625 to 0.15625
- bias_contract: bfloat16 [2, 768], P('section', 'fsdp'), may hold values from -2 to 2
Outputs:
- section_outputs: bfloat16 [2, 2, 16, 640, 768], P('section', None, ('fsdp', 'rep'))
- section_input_grads: bfloat16 [2, 2, 16, 640, 768], P('section', None, ('fsdp', 'rep'))
- gain_one_grad: float32 [2, 768], P('section', 'fsdp')
- shift_one_grad: float32 [2, 768], P('section', 'fsdp')
- project_grad: float32 [2, 768, 2304], P('section', 'fsdp')
- bias_query_grad: float32 [2, 768], P('section', 'fsdp')
- bias_value_grad: float32 [2, 768], P('section', 'fsdp')
- output_grad: float32 [2, 768, 768], P('section', 'fsdp')
- bias_output_grad: float32 [2, 768], P('section', 'fsdp')
- gain_two_grad: float32 [2, 768], P('section', 'fsdp')
- shift_two_grad: float32 [2, 768], P('section', 'fsdp')
- expand_grad: float32 [2, 768, 3072], P('section', 'fsdp')
- bias_expand_grad: float32 [2, 3072], P('section', 'fsdp')
- contract_grad: float32 [2, 3072, 768], P('section', 'fsdp')
- bias_contract_grad: float32 [2, 768], P('section', 'fsdp')
The draws below stay inside these ranges and needn't reach their ends.
Inputs may be any that keep to these rules, and one draw needn't show every extreme that they name: `live_slots`: some micro-batch has all 16 slots live.
All inputs are finite; a program needn't handle non-finite values.
Results may differ from the reference program's by a relative error of at most 0.018.
Values may be sent and summed in bfloat16 or wider, within the bound.
No kernel may reach another device: no remote copies, remote signals or barrier semaphores. Data moves between devices by JAX's collectives and lax.ppermute only.
A program may use at most 448 MiB of HBM per device.

```python
import jax
import jax.numpy as jnp
from jax import lax

D = 768
HEADS = 12
HD = 64
FF = 3072
LEN = 640
MICRO = 2
SLOTS = 16


def draw_live_slots(key, part):
    key = jax.random.fold_in(key, 7)
    slot_key = jax.random.fold_in(key, 11)
    full_key = jax.random.fold_in(key, 13)
    drawn = jax.random.randint(slot_key, (MICRO, SLOTS), 0, 4, dtype=jnp.int32)
    live = jnp.where(drawn > 0, 1, 0).astype(jnp.int32)
    full_position = jax.random.randint(full_key, (), 0, MICRO, dtype=jnp.int32)
    position = jnp.arange(MICRO, dtype=jnp.int32)
    return jnp.where((position == full_position)[:, None], 1, live).astype(jnp.int32)


def spiked(entries, own_key, source, target, parts, factor):
    def block_of(dim):
        return (jnp.arange(entries.shape[dim]) // (entries.shape[dim] // parts)).reshape((-1,) + (1,) * (entries.ndim - 1 - dim))

    one_side = jax.random.permutation(own_key, parts)[block_of(target)]
    far = (block_of(target) + parts // 2) % parts
    return jnp.where((block_of(source) == one_side) | (block_of(source) == far), factor * entries, entries)


def block_scale(key, shape, shards, least, high):
    def one(dim, parts):
        heights = jax.random.uniform(jax.random.fold_in(jax.random.fold_in(key, 6), dim), (parts,), jnp.float32, least / len(shards), high / len(shards))
        return jnp.repeat(jnp.exp(heights), shape[dim] // parts).reshape((-1,) + (1,) * (len(shape) - dim - 1))

    level = one(*shards[0])
    for cut in shards[1:]:
        level = level * one(*cut)
    return level


def bell_draw(key, shape, width, bound, split=(), kind=jnp.bfloat16):
    entries = jax.random.normal(key, shape, jnp.float32) * width
    if len(split) > 0:
        entries = block_scale(key, shape, split, -0.22, 0.18) * entries
    return jnp.clip(entries, min=-bound, max=bound).astype(kind)


def gaussian_with(rng, shape, scale, reach, pieces, heavy, kind=jnp.bfloat16):
    values = scale * jax.random.normal(rng, shape, jnp.float32)
    if pieces:
        values = values * block_scale(rng, shape, pieces, -0.22, 0.18)
    return jnp.clip(spiked(values, jax.random.fold_in(rng, 3), *heavy), -reach, reach).astype(kind)


def setup_inputs(seed: int = 0) -> dict:
    key_of = jax.random.split(jax.random.key(seed), 17)
    return {
        "inputs": gaussian_with(key_of[0], (MICRO, SLOTS, LEN, D), 1.0, 6.0, ((1, 16),), (1, 3, 16, 2.0)),
        "cotangent": bell_draw(key_of[1], (MICRO, SLOTS, LEN, D), 1.0, 6.0, ((1, 16),)),
        "live_slots": draw_live_slots(jax.random.fold_in(key_of[16], 71), 0),
        "gain_one": jnp.clip(1.0 + 0.1 * jax.random.normal(key_of[3], (2, D), jnp.float32), 0.5, 1.5).astype(jnp.bfloat16),
        "shift_one": bell_draw(key_of[4], (2, D), 0.3, 2.0, ((0, 2), (1, 4))),
        "project": bell_draw(key_of[5], (2, D, 3 * D), D ** -0.5, 0.21875, ((0, 2), (1, 4))),
        "bias_query": bell_draw(key_of[6], (2, D), 0.5, 3.0, ((0, 2), (1, 4))),
        "bias_value": bell_draw(key_of[7], (2, D), 0.3, 2.0, ((0, 2), (1, 4))),
        "output": bell_draw(key_of[8], (2, D, D), (max(1, D * 3 // LEN)) ** -0.5, 3.5, ((0, 2), (1, 4))),
        "bias_output": bell_draw(key_of[9], (2, D), 0.3, 2.0, ((0, 2), (1, 4))),
        "gain_two": jnp.clip(1.0 + 0.1 * jax.random.normal(key_of[10], (2, D), jnp.float32), 0.5, 1.5).astype(jnp.bfloat16),
        "shift_two": bell_draw(key_of[11], (2, D), 0.3, 2.0, ((0, 2), (1, 4))),
        "expand": bell_draw(key_of[12], (2, D, FF), D ** -0.5, 0.21875, ((0, 2), (1, 4))),
        "bias_expand": bell_draw(key_of[13], (2, FF), 0.5, 3.0, ((0, 2), (1, 4))),
        "contract": bell_draw(key_of[14], (2, FF, D), (FF // 2) ** -0.5, 0.15625, ((0, 2), (1, 4))),
        "bias_contract": bell_draw(key_of[15], (2, D), 0.3, 2.0, ((0, 2), (1, 4))),
    }


epsilon = 1e-05

@jax.custom_vjp
def low(v):
    return lax.optimization_barrier(v.astype(jnp.bfloat16)).astype(jnp.float32)

@jax.custom_vjp
def low_back(v):
    return v

def low_keep(v):
    return (low(v), None)

def low_pass(kept, grad):
    return (grad,)

def back_keep(v):
    return (v, None)

def back_low(kept, grad):
    return (low(grad),)
low.defvjp(low_keep, low_pass)
low_back.defvjp(back_keep, back_low)

def norm_rows(values_in, gain, shift_in):
    mean_row = lax.optimization_barrier(jnp.mean(values_in, axis=-1, keepdims=True))
    centered = values_in - mean_row
    factor = lax.rsqrt(lax.optimization_barrier(jnp.mean(centered * centered, axis=-1, keepdims=True)) + epsilon)
    return centered * factor * gain + shift_in

def attend(queries, key_rows, value_rows):
    query_heads = queries.reshape(LEN, HEADS, HD).transpose(1, 0, 2)
    key_heads = key_rows.reshape(LEN, HEADS, HD).transpose(1, 0, 2)
    value_heads = value_rows.reshape(LEN, HEADS, HD).transpose(1, 0, 2)
    scores = jnp.einsum('hqd,hkd->hqk', query_heads, key_heads, precision=lax.Precision.HIGHEST) * HD ** (-0.5)
    scores = low_back(scores)
    probs_low = low(jax.nn.softmax(scores, axis=-1))
    context = jnp.einsum('hqk,hkd->hqd', probs_low, value_heads, precision=lax.Precision.HIGHEST)
    return context.transpose(1, 0, 2).reshape(LEN, HEADS * HD)

def clip_layer(params, clip_in):
    gain_one, shift_one, project, bias_query, bias_value, output, bias_output, gain_two, shift_two, expand, bias_expand, contract, bias_contract = params
    normed = low(norm_rows(clip_in, gain_one, shift_one))
    projected = jnp.dot(normed, project, precision=lax.Precision.HIGHEST)
    queries = low_back(low(projected[:, :D] + bias_query))
    key_rows = low_back(low(projected[:, D:2 * D]))
    value_rows = low_back(low(projected[:, 2 * D:] + bias_value))
    context = low_back(low(attend(queries, key_rows, value_rows)))
    attended = low_back(jnp.dot(context, output, precision=lax.Precision.HIGHEST) + bias_output)
    hidden = clip_in + attended
    mixed_rows = low(norm_rows(hidden, gain_two, shift_two))
    upper_pre = low_back(jnp.dot(mixed_rows, expand, precision=lax.Precision.HIGHEST) + bias_expand)
    active = low(jax.nn.gelu(upper_pre, approximate=False))
    lowered = low_back(jnp.dot(active, contract, precision=lax.Precision.HIGHEST) + bias_contract)
    return low(hidden + lowered)

def run_layers(first, second, clip_rows, shift_zero):
    middle = lax.map(jax.checkpoint(lambda clip_in: clip_layer(first, clip_in)), clip_rows)
    entering = low_back(middle + shift_zero)
    final = lax.map(jax.checkpoint(lambda clip_in: clip_layer(second, clip_in)), entering)
    return (middle, final)

def reference(inputs, cotangent, live_slots, gain_one, shift_one, project, bias_query, bias_value, output, bias_output, gain_two, shift_two, expand, bias_expand, contract, bias_contract):
    stacked = (gain_one, shift_one, project, bias_query, bias_value, output, bias_output, gain_two, shift_two, expand, bias_expand, contract, bias_contract)
    first = tuple((item[0].astype(jnp.float32) for item in stacked))
    second = tuple((item[1].astype(jnp.float32) for item in stacked))
    live_mask = live_slots.astype(jnp.float32)
    live_cot = cotangent.astype(jnp.float32) * live_mask[:, :, None, None]
    clip_rows = inputs.astype(jnp.float32).reshape(MICRO * SLOTS, LEN, D)
    shift_zero = jnp.zeros_like(clip_rows)
    (middle, final), pullback = jax.vjp(run_layers, first, second, clip_rows, shift_zero)
    grad_first, grad_second, grad_inputs, grad_middle = pullback((jnp.zeros_like(middle), live_cot.reshape(MICRO * SLOTS, LEN, D)))
    shape_out = (2, MICRO, SLOTS, LEN, D)
    section_outputs = jnp.stack([middle, final]).reshape(shape_out).astype(jnp.bfloat16)
    section_input_grads = jnp.stack([grad_inputs, grad_middle]).reshape(shape_out).astype(jnp.bfloat16)
    grads = tuple((jnp.stack([one_grad, two_grad]) for one_grad, two_grad in zip(grad_first, grad_second)))
    return (section_outputs, section_input_grads, grads[0], grads[1], grads[2], grads[3], grads[4], grads[5], grads[6], grads[7], grads[8], grads[9], grads[10], grads[11], grads[12])
```

```python
import math

import jax
import jax.numpy as jnp
from jax import lax
from jax.experimental import pallas as pl
from jax.experimental.pallas import tpu as pltpu
from jax.sharding import PartitionSpec as P

HEADS = 12
HD = 64
PAIR = 2 * HD
SCALE = HD ** (-0.5)
epsilon = 1e-05
LOW = jnp.bfloat16
FULL = jnp.float32


def matmul(left, right):
    return jnp.dot(left, right, preferred_element_type=FULL)


def matmul_left(left, right):
    return lax.dot_general(left, right, (((0,), (0,)), ((), ())), preferred_element_type=FULL)


def matmul_right(left, right):
    return lax.dot_general(left, right, (((1,), (1,)), ((), ())), preferred_element_type=FULL)


def row_stats(values_in):
    mean_row = jnp.mean(values_in, axis=-1, keepdims=True)
    centered = values_in - mean_row
    factor = lax.rsqrt(jnp.mean(centered * centered, axis=-1, keepdims=True) + epsilon)
    return (centered * factor, factor)


def norm_back(grad_norm, normal, factor):
    first_mean = jnp.mean(grad_norm, axis=-1, keepdims=True)
    second_mean = jnp.mean(grad_norm * normal, axis=-1, keepdims=True)
    return factor * (grad_norm - first_mean - normal * second_mean)


def head_mask(head):
    lanes = lax.broadcasted_iota(jnp.int32, (1, PAIR), 1)
    return (lanes >= head * HD) & (lanes < (head + 1) * HD)


def only_head(rows, head):
    return jnp.where(head_mask(head), rows, jnp.zeros_like(rows))


def attend_kernel(q_ref, k_ref, v_ref, context_ref, lse_ref):
    queries = q_ref[...]
    keys = k_ref[...] * jnp.asarray(SCALE, LOW)
    values_t = v_ref[...].T
    pieces = []
    for head in range(2):
        scores = matmul_right(only_head(keys, head), queries)
        top = jnp.max(scores, axis=0, keepdims=True)
        exponent = jnp.exp(scores - top)
        total = jnp.sum(exponent, axis=0, keepdims=True)
        lse_ref[0, head : head + 1, :] = top + jnp.log(total)
        part = matmul(values_t[head * HD : (head + 1) * HD], exponent.astype(LOW))
        pieces.append(part * (1.0 / total))
    context_ref[...] = jnp.concatenate(pieces, 0).T.astype(LOW)


def attend_back_kernel(q_ref, k_ref, v_ref, lse_ref, g_ref, dq_ref, dk_ref, dv_ref):
    scale = jnp.asarray(SCALE, LOW)
    queries = q_ref[...]
    keys = k_ref[...] * scale
    values = v_ref[...]
    grads = g_ref[...]
    scaled_queries = queries * scale
    keys_t = keys.T
    pieces = []
    key_grad = None
    value_grad = None
    for head in range(2):
        grad_head = only_head(grads, head)
        scores = matmul_right(only_head(keys, head), queries)
        probs = jnp.exp(scores - lse_ref[0, head : head + 1, :])
        grad_probs = matmul_right(values, grad_head)
        value_part = matmul(probs.astype(LOW), grad_head)
        inner = jnp.sum(probs * grad_probs, axis=0, keepdims=True)
        grad_scores = (probs * (grad_probs - inner)).astype(LOW)
        key_part = matmul(grad_scores, only_head(scaled_queries, head))
        pieces.append(matmul(keys_t[head * HD : (head + 1) * HD], grad_scores))
        key_grad = key_part if key_grad is None else key_grad + key_part
        value_grad = value_part if value_grad is None else value_grad + value_part
    dq_ref[...] = jnp.concatenate(pieces, 0).T.astype(LOW)
    dk_ref[...] = key_grad.astype(LOW)
    dv_ref[...] = value_grad.astype(LOW)


def attend_cost(rows, length, products):
    return pl.CostEstimate(
        flops=2 * products * rows * length * HEADS * HD * 3,
        bytes_accessed=rows * HEADS * HD * 2 * (products + 2),
        transcendentals=rows * length * HEADS,
    )


def attend_forward(clips, length, queries, key_rows, value_rows):
    rows, width = queries.shape
    pairs = width // PAIR
    block = pl.BlockSpec((length, PAIR), lambda c, j: (c, j))
    lse_block = pl.BlockSpec((1, 8, length), lambda c, j: (c * pairs + j, 0, 0))
    return pl.pallas_call(
        attend_kernel,
        grid=(clips, pairs),
        in_specs=[block] * 3,
        out_specs=[block, lse_block],
        out_shape=[
            jax.ShapeDtypeStruct((rows, width), LOW),
            jax.ShapeDtypeStruct((clips * pairs, 8, length), FULL),
        ],
        compiler_params=pltpu.CompilerParams(vmem_limit_bytes=40 * 1024 * 1024),
        cost_estimate=attend_cost(rows, length, 2),
        name="attend_forward",
    )(queries, key_rows, value_rows)


def attend_backward(clips, length, queries, key_rows, value_rows, lse, grad_context):
    rows, width = queries.shape
    pairs = width // PAIR
    block = pl.BlockSpec((length, PAIR), lambda c, j: (c, j))
    lse_block = pl.BlockSpec((1, 8, length), lambda c, j: (c * pairs + j, 0, 0))
    return pl.pallas_call(
        attend_back_kernel,
        grid=(clips, pairs),
        in_specs=[block] * 3 + [lse_block, block],
        out_specs=[block] * 3,
        out_shape=[jax.ShapeDtypeStruct((rows, width), LOW)] * 3,
        compiler_params=pltpu.CompilerParams(vmem_limit_bytes=48 * 1024 * 1024),
        cost_estimate=attend_cost(rows, length, 5),
        name="attend_backward",
    )(queries, key_rows, value_rows, lse, grad_context)


def gelu_parts(upper):
    size = jnp.abs(upper)
    turn = 1.0 / (1.0 + (0.3275911 / math.sqrt(2.0)) * size)
    bell = jnp.exp(-0.5 * upper * upper)
    series = turn * (
        0.5 * 0.254829592
        + turn
        * (
            0.5 * -0.284496736
            + turn * (0.5 * 1.421413741 + turn * (0.5 * -1.453152027 + turn * (0.5 * 1.061405429)))
        )
    )
    tail = series * bell
    below = jnp.where(upper < 0, tail, 1.0 - tail)
    return upper * below, below + upper * bell * (1.0 / math.sqrt(2.0 * math.pi))


def layer_forward(weights, clips, length, rows_in):
    width = rows_in.shape[1]
    token_rows = rows_in.astype(FULL)
    normal_one, _ = row_stats(token_rows)
    normed = (normal_one * weights["gain_one"] + weights["shift_one"]).astype(LOW)
    projected = matmul(normed, weights["project"])
    queries = (projected[:, :width] + weights["bias_query"]).astype(LOW)
    key_rows = projected[:, width : 2 * width].astype(LOW)
    value_rows = (projected[:, 2 * width :] + weights["bias_value"]).astype(LOW)
    context, lse = attend_forward(clips, length, queries, key_rows, value_rows)
    hidden = token_rows + (matmul(context, weights["output"]) + weights["bias_output"])
    normal_two, _ = row_stats(hidden)
    mixed_rows = (normal_two * weights["gain_two"] + weights["shift_two"]).astype(LOW)
    upper = matmul(mixed_rows, weights["expand"]) + weights["bias_expand"]
    active, slope = gelu_parts(upper)
    active = active.astype(LOW)
    slope = slope.astype(LOW)
    result = (hidden + (matmul(active, weights["contract"]) + weights["bias_contract"])).astype(LOW)
    kept = (rows_in, normed, queries, key_rows, value_rows, lse, context, hidden, mixed_rows, active, slope)
    return result, kept


def layer_backward(weights, clips, length, kept, grad_low, grad_full):
    rows_in, normed, queries, key_rows, value_rows, lse, context, hidden, mixed_rows, active, slope = kept
    grad_upper = (matmul_right(grad_low, weights["contract"]) * slope).astype(LOW)
    grad_mixed = matmul_right(grad_upper, weights["expand"])
    normal_two, factor_two = row_stats(hidden)
    gain_two_grad = jnp.sum(grad_mixed * normal_two, axis=0)
    shift_two_grad = jnp.sum(grad_mixed, axis=0)
    grad_hidden = grad_full + norm_back(grad_mixed * weights["gain_two"], normal_two, factor_two)
    grad_attended = grad_hidden.astype(LOW)
    grad_context = matmul_right(grad_attended, weights["output"]).astype(LOW)
    grad_queries, grad_keys, grad_values = attend_backward(
        clips, length, queries, key_rows, value_rows, lse, grad_context
    )
    grad_proj = jnp.concatenate([grad_queries, grad_keys, grad_values], 1)
    grad_normed = matmul_right(grad_proj, weights["project"])
    normal_one, factor_one = row_stats(rows_in.astype(FULL))
    gain_one_grad = jnp.sum(grad_normed * normal_one, axis=0)
    shift_one_grad = jnp.sum(grad_normed, axis=0)
    grad_in = grad_hidden + norm_back(grad_normed * weights["gain_one"], normal_one, factor_one)

    def total(part):
        return jnp.sum(part.astype(FULL), axis=0)

    small = dict(
        gain_one=gain_one_grad,
        shift_one=shift_one_grad,
        bias_query=total(grad_queries),
        bias_value=total(grad_values),
        bias_output=total(grad_attended),
        gain_two=gain_two_grad,
        shift_two=shift_two_grad,
        bias_expand=total(grad_upper),
        bias_contract=total(grad_low),
    )
    factors = dict(
        contract=(active, grad_low),
        expand=(mixed_rows, grad_upper),
        output=(context, grad_attended),
        project=(normed, grad_proj),
    )
    return grad_in.astype(LOW), small, factors


SMALL = (
    "gain_one",
    "shift_one",
    "bias_query",
    "bias_value",
    "bias_output",
    "gain_two",
    "shift_two",
    "bias_contract",
    "bias_expand",
)
LARGE = ("project", "output", "expand", "contract")
ORDER = (
    "gain_one",
    "shift_one",
    "project",
    "bias_query",
    "bias_value",
    "output",
    "bias_output",
    "gain_two",
    "shift_two",
    "expand",
    "bias_expand",
    "contract",
    "bias_contract",
)


def gather_weights(shards):
    weights = {}
    packed = jnp.concatenate([shards[name] for name in SMALL], 0)[None]
    spread = lax.all_gather(packed, "fsdp", axis=0, tiled=True)
    place = 0
    for name in SMALL:
        size = shards[name].shape[0]
        weights[name] = spread[:, place : place + size].reshape(-1).astype(FULL)
        place += size
    for name in LARGE:
        weights[name] = lax.all_gather(shards[name], "fsdp", axis=0, tiled=True)
    return weights


def reduce_large(grad):
    owned = lax.psum_scatter(grad.astype(LOW), "fsdp", scatter_dimension=0, tiled=True)
    return lax.psum(owned, "rep").astype(FULL)


def reduce_small(small, shards):
    packed = jnp.concatenate([small[name] for name in SMALL], 0)
    whole = lax.psum(packed.reshape(-1, 128), ("fsdp", "rep")).reshape(-1)
    index = lax.axis_index("fsdp")
    place = 0
    owned = {}
    for name in SMALL:
        size = small[name].shape[0]
        part = shards[name].shape[0]
        owned[name] = lax.dynamic_slice_in_dim(whole[place : place + size], index * part, part)
        place += size
    return owned


def local(inputs, cotangent, live_slots, *params):
    shards = {name: part[0] for name, part in zip(ORDER, params)}
    micro_count, clips, length, width = inputs.shape
    rows = clips * length
    first = lax.axis_index("section") == 0
    inputs = inputs.reshape(micro_count, rows, width)
    live = jnp.repeat(live_slots.reshape(micro_count, clips, 1), length, axis=1)
    cotangent = cotangent.reshape(micro_count, rows, width) * (live == 1).astype(LOW)
    weights = gather_weights(shards)

    def forward(rows_in):
        return layer_forward(weights, clips, length, rows_in)

    def onward(rows_out):
        return lax.ppermute(rows_out, "section", [(0, 1)])

    def back(grad_rows):
        return lax.ppermute(grad_rows, "section", [(1, 0)])

    out_a, _ = forward(inputs[0])
    out_b, kept_odd = forward(jnp.where(first, inputs[1], onward(out_a)))
    out_c, kept_even = forward(jnp.where(first, inputs[0], onward(out_b)))
    section_outputs = jnp.stack([jnp.where(first, out_c, out_b), jnp.where(first, out_b, out_c)])

    def backward(kept, grad_low):
        return layer_backward(weights, clips, length, kept, grad_low, grad_low.astype(FULL))

    grad_a, _, _ = backward(kept_odd, cotangent[0])
    grad_b, small_b, factors_b = backward(kept_even, jnp.where(first, back(grad_a), cotangent[1]))
    grad_c, small_c, factors_c = backward(kept_odd, jnp.where(first, back(grad_b), cotangent[0]))
    section_input_grads = jnp.stack([jnp.where(first, grad_b, grad_c), jnp.where(first, grad_c, grad_b)])

    owned = {}
    for name in ("contract", "expand", "output", "project"):
        (left_b, right_b), (left_c, right_c) = factors_b[name], factors_c[name]
        left = jnp.concatenate([left_b, left_c], 0)
        right = jnp.concatenate([right_b, right_c], 0)
        owned[name] = reduce_large(matmul_left(left, right))
    small = {name: small_b[name] + small_c[name] for name in SMALL}
    owned.update(reduce_small(small, shards))
    shape_out = (1, micro_count, clips, length, width)
    return (
        section_outputs.reshape(shape_out),
        section_input_grads.reshape(shape_out),
    ) + tuple(owned[name][None] for name in ORDER)


def solution(mesh):
    rows_spec = P(None, ("fsdp", "rep"), None, None)
    vector = P("section", "fsdp")
    matrix = P("section", "fsdp", None)
    params = tuple(matrix if name in LARGE else vector for name in ORDER)
    in_specs = (rows_spec, rows_spec, P(None, ("fsdp", "rep"))) + params
    out_rows = P("section", None, ("fsdp", "rep"), None, None)
    out_specs = (out_rows, out_rows) + params
    return jax.shard_map(local, mesh=mesh, in_specs=in_specs, out_specs=out_specs, check_vma=False)
```

```python
import math

import jax
import jax.numpy as jnp
from jax import lax
from jax.experimental import pallas as pl
from jax.experimental.pallas import tpu as pltpu
from jax.sharding import PartitionSpec as P

HEADS = 12
HD = 64
PAIR = 2 * HD
SCALE = HD ** (-0.5)
epsilon = 1e-05
LOW = jnp.bfloat16
FULL = jnp.float32
BRIEF = pl.CostEstimate(flops=1024, bytes_accessed=1024, transcendentals=0)


def matmul(left, right):
    return jnp.dot(left, right, preferred_element_type=FULL)


def matmul_left(left, right):
    return lax.dot_general(left, right, (((0,), (0,)), ((), ())), preferred_element_type=FULL)


def matmul_right(left, right):
    return lax.dot_general(left, right, (((1,), (1,)), ((), ())), preferred_element_type=FULL)


def row_stats(values_in):
    mean_row = jnp.mean(values_in, axis=-1, keepdims=True)
    centered = values_in - mean_row
    factor = lax.rsqrt(jnp.mean(centered * centered, axis=-1, keepdims=True) + epsilon)
    return (centered * factor, factor)


def norm_back(grad_norm, normal, factor):
    first_mean = jnp.mean(grad_norm, axis=-1, keepdims=True)
    second_mean = jnp.mean(grad_norm * normal, axis=-1, keepdims=True)
    return factor * (grad_norm - first_mean - normal * second_mean)


def head_mask(head):
    lanes = lax.broadcasted_iota(jnp.int32, (1, PAIR), 1)
    return (lanes >= head * HD) & (lanes < (head + 1) * HD)


def only_head(rows, head):
    return jnp.where(head_mask(head), rows, jnp.zeros_like(rows))


def attend_kernel(q_ref, k_ref, v_ref, context_ref, lse_ref):
    queries = q_ref[...]
    keys = k_ref[...] * jnp.asarray(SCALE, LOW)
    values_t = v_ref[...].T
    pieces = []
    for head in range(2):
        scores = matmul_right(only_head(keys, head), queries)
        top = jnp.max(scores, axis=0, keepdims=True)
        exponent = jnp.exp(scores - top)
        total = jnp.sum(exponent, axis=0, keepdims=True)
        lse_ref[0, head : head + 1, :] = top + jnp.log(total)
        part = matmul(values_t[head * HD : (head + 1) * HD], exponent.astype(LOW))
        pieces.append(part * (1.0 / total))
    context_ref[...] = jnp.concatenate(pieces, 0).T.astype(LOW)


def attend_back_kernel(q_ref, k_ref, v_ref, lse_ref, g_ref, dq_ref, dk_ref, dv_ref):
    scale = jnp.asarray(SCALE, LOW)
    queries = q_ref[...]
    keys = k_ref[...] * scale
    values = v_ref[...]
    grads = g_ref[...]
    scaled_queries = queries * scale
    keys_t = keys.T
    pieces = []
    key_grad = None
    value_grad = None
    for head in range(2):
        grad_head = only_head(grads, head)
        scores = matmul_right(only_head(keys, head), queries)
        probs = jnp.exp(scores - lse_ref[0, head : head + 1, :])
        grad_probs = matmul_right(values, grad_head)
        value_part = matmul(probs.astype(LOW), grad_head)
        inner = jnp.sum(probs * grad_probs, axis=0, keepdims=True)
        grad_scores = (probs * (grad_probs - inner)).astype(LOW)
        key_part = matmul(grad_scores, only_head(scaled_queries, head))
        pieces.append(matmul(keys_t[head * HD : (head + 1) * HD], grad_scores))
        key_grad = key_part if key_grad is None else key_grad + key_part
        value_grad = value_part if value_grad is None else value_grad + value_part
    dq_ref[...] = jnp.concatenate(pieces, 0).T.astype(LOW)
    dk_ref[...] = key_grad.astype(LOW)
    dv_ref[...] = value_grad.astype(LOW)


def ffn_up_kernel(mixed_ref, expand_ref, bias_ref, active_ref, slope_ref):
    rows = mixed_ref.shape[0]
    part = rows // 4
    bias = bias_ref[...]
    for piece in range(4):
        span = pl.ds(piece * part, part)
        upper = matmul(mixed_ref[span, :], expand_ref[...]) + bias
        active, slope = gelu_parts(upper)
        active_ref[span, :] = active.astype(LOW)
        slope_ref[span, :] = slope.astype(LOW)


def ffn_up(mixed_rows, expand, bias):
    rows, width = mixed_rows.shape
    hidden_units = expand.shape[1]
    step = 512
    block = pl.BlockSpec((rows, step), lambda j: (0, j))
    return pl.pallas_call(
        ffn_up_kernel,
        grid=(hidden_units // step,),
        in_specs=[
            pl.BlockSpec((rows, width), lambda j: (0, 0)),
            pl.BlockSpec((width, step), lambda j: (0, j)),
            pl.BlockSpec((1, step), lambda j: (0, j)),
        ],
        out_specs=[block, block],
        out_shape=[jax.ShapeDtypeStruct((rows, hidden_units), LOW)] * 2,
        compiler_params=pltpu.CompilerParams(vmem_limit_bytes=40 * 1024 * 1024),
        cost_estimate=BRIEF,
        name="ffn_up",
    )(mixed_rows, expand, bias.reshape(1, hidden_units))


def ffn_whole_kernel(
    mixed_ref, expand_ref, bias_ref, contract_ref, hidden_ref, out_bias_ref, active_ref, slope_ref, result_ref, total_ref
):
    step = pl.program_id(0)

    @pl.when(step == 0)
    def _():
        total_ref[...] = hidden_ref[...] + out_bias_ref[...]

    rows = mixed_ref.shape[0]
    part = rows // 4
    bias = bias_ref[...]
    for piece in range(4):
        span = pl.ds(piece * part, part)
        upper = matmul(mixed_ref[span, :], expand_ref[...]) + bias
        active, slope = gelu_parts(upper)
        active = active.astype(LOW)
        active_ref[span, :] = active
        slope_ref[span, :] = slope.astype(LOW)
        total_ref[span, :] += matmul(active, contract_ref[...])

    @pl.when(step == pl.num_programs(0) - 1)
    def _():
        result_ref[...] = total_ref[...].astype(LOW)


def ffn_whole(mixed_rows, expand, bias, contract, hidden, out_bias):
    rows, width = mixed_rows.shape
    hidden_units = expand.shape[1]
    step = 512
    block = pl.BlockSpec((rows, step), lambda j: (0, j))
    whole = pl.BlockSpec((rows, width), lambda j: (0, 0))
    return pl.pallas_call(
        ffn_whole_kernel,
        grid=(hidden_units // step,),
        in_specs=[
            whole,
            pl.BlockSpec((width, step), lambda j: (0, j)),
            pl.BlockSpec((1, step), lambda j: (0, j)),
            pl.BlockSpec((step, width), lambda j: (j, 0)),
            whole,
            pl.BlockSpec((1, width), lambda j: (0, 0)),
        ],
        out_specs=[block, block, whole],
        out_shape=[
            jax.ShapeDtypeStruct((rows, hidden_units), LOW),
            jax.ShapeDtypeStruct((rows, hidden_units), LOW),
            jax.ShapeDtypeStruct((rows, width), LOW),
        ],
        scratch_shapes=[pltpu.VMEM((rows, width), FULL)],
        compiler_params=pltpu.CompilerParams(vmem_limit_bytes=44 * 1024 * 1024),
        cost_estimate=BRIEF,
        name="ffn_whole",
    )(mixed_rows, expand, bias.reshape(1, hidden_units), contract, hidden, out_bias.reshape(1, width))


def ffn_back_kernel(grad_ref, contract_ref, slope_ref, expand_ref, upper_ref, mixed_ref, sum_ref):
    @pl.when(pl.program_id(0) == 0)
    def _():
        mixed_ref[...] = jnp.zeros_like(mixed_ref)

    rows = grad_ref.shape[0]
    part = rows // 2
    total = None
    for piece in range(2):
        span = pl.ds(piece * part, part)
        grad_active = matmul_right(grad_ref[span, :], contract_ref[...])
        grad_upper = (grad_active * slope_ref[span, :].astype(FULL)).astype(LOW)
        upper_ref[span, :] = grad_upper
        column = jnp.sum(grad_upper.astype(FULL), axis=0, keepdims=True)
        total = column if total is None else total + column
        mixed_ref[span, :] += matmul_right(grad_upper, expand_ref[...])
    sum_ref[...] = total


def ffn_back(grad_low, contract, slope, expand):
    rows, width = grad_low.shape
    hidden_units = contract.shape[0]
    step = 512
    block = pl.BlockSpec((rows, step), lambda j: (0, j))
    whole = pl.BlockSpec((rows, width), lambda j: (0, 0))
    return pl.pallas_call(
        ffn_back_kernel,
        grid=(hidden_units // step,),
        in_specs=[
            whole,
            pl.BlockSpec((step, width), lambda j: (j, 0)),
            block,
            pl.BlockSpec((width, step), lambda j: (0, j)),
        ],
        out_specs=[block, whole, pl.BlockSpec((1, step), lambda j: (0, j))],
        out_shape=[
            jax.ShapeDtypeStruct((rows, hidden_units), LOW),
            jax.ShapeDtypeStruct((rows, width), FULL),
            jax.ShapeDtypeStruct((1, hidden_units), FULL),
        ],
        compiler_params=pltpu.CompilerParams(vmem_limit_bytes=40 * 1024 * 1024),
        cost_estimate=BRIEF,
        name="ffn_back",
    )(grad_low, contract, slope, expand)


def attend_forward(clips, length, queries, key_rows, value_rows):
    rows, width = queries.shape
    pairs = width // PAIR
    block = pl.BlockSpec((length, PAIR), lambda c, j: (c, j))
    lse_block = pl.BlockSpec((1, 8, length), lambda c, j: (c * pairs + j, 0, 0))
    return pl.pallas_call(
        attend_kernel,
        grid=(clips, pairs),
        in_specs=[block] * 3,
        out_specs=[block, lse_block],
        out_shape=[
            jax.ShapeDtypeStruct((rows, width), LOW),
            jax.ShapeDtypeStruct((clips * pairs, 8, length), FULL),
        ],
        compiler_params=pltpu.CompilerParams(vmem_limit_bytes=40 * 1024 * 1024),
        cost_estimate=BRIEF,
        name="attend_forward",
    )(queries, key_rows, value_rows)


def attend_backward(clips, length, queries, key_rows, value_rows, lse, grad_context, low=0, high=None):
    rows, width = queries.shape
    pairs = width // PAIR
    high = pairs if high is None else high
    block = pl.BlockSpec((length, PAIR), lambda c, j: (c, low + j))
    lse_block = pl.BlockSpec((1, 8, length), lambda c, j: (c * pairs + low + j, 0, 0))
    out_block = pl.BlockSpec((length, PAIR), lambda c, j: (c, j))
    return pl.pallas_call(
        attend_back_kernel,
        grid=(clips, high - low),
        in_specs=[block] * 3 + [lse_block, block],
        out_specs=[out_block] * 3,
        out_shape=[jax.ShapeDtypeStruct((rows, (high - low) * PAIR), LOW)] * 3,
        compiler_params=pltpu.CompilerParams(vmem_limit_bytes=48 * 1024 * 1024),
        cost_estimate=BRIEF,
        name="attend_backward",
    )(queries, key_rows, value_rows, lse, grad_context)


def gelu_parts(upper):
    size = jnp.abs(upper)
    turn = 1.0 / (1.0 + (0.3275911 / math.sqrt(2.0)) * size)
    bell = jnp.exp(-0.5 * upper * upper)
    series = turn * (
        0.5 * 0.254829592
        + turn
        * (
            0.5 * -0.284496736
            + turn * (0.5 * 1.421413741 + turn * (0.5 * -1.453152027 + turn * (0.5 * 1.061405429)))
        )
    )
    tail = series * bell
    below = jnp.where(upper < 0, tail, 1.0 - tail)
    return upper * below, below + upper * bell * (1.0 / math.sqrt(2.0 * math.pi))


def layer_forward(weights, clips, length, rows_in, begin=None, before=None, after=None, last=None):
    width = rows_in.shape[1]
    token_rows = rows_in.astype(FULL)
    normal_one, _ = row_stats(token_rows)
    normed = (normal_one * weights["gain_one"] + weights["shift_one"]).astype(LOW)
    if begin is not None:
        normed = begin(normed)
    projected = matmul(normed, weights["project"])
    queries = (projected[:, :width] + weights["bias_query"]).astype(LOW)
    key_rows = projected[:, width : 2 * width].astype(LOW)
    value_rows = (projected[:, 2 * width :] + weights["bias_value"]).astype(LOW)
    if before is not None:
        queries = before(queries)
    context, lse = attend_forward(clips, length, queries, key_rows, value_rows)
    if after is not None:
        context = after(context)
    hidden = token_rows + (matmul(context, weights["output"]) + weights["bias_output"])
    normal_two, _ = row_stats(hidden)
    mixed_rows = (normal_two * weights["gain_two"] + weights["shift_two"]).astype(LOW)
    if last is not None:
        active, slope = ffn_up(mixed_rows, weights["expand"], weights["bias_expand"])
        active = last(active)
        result = (hidden + (matmul(active, weights["contract"]) + weights["bias_contract"])).astype(LOW)
    else:
        active, slope, result = ffn_whole(
            mixed_rows,
            weights["expand"],
            weights["bias_expand"],
            weights["contract"],
            hidden,
            weights["bias_contract"],
        )
    kept = (rows_in, normed, queries, key_rows, value_rows, lse, context, hidden, mixed_rows, active, slope)
    return result, kept


def tie(value, *others):
    return lax.optimization_barrier((value,) + others)[0]


def layer_backward(weights, clips, length, kept, grad_low, weight_grad):
    rows_in, normed, queries, key_rows, value_rows, lse, context, hidden, mixed_rows, active, slope = kept
    grad_full = grad_low.astype(FULL)
    grad_low = weight_grad("contract", active, grad_low, grad_low)
    grad_upper, grad_mixed, bias_expand_grad = ffn_back(
        grad_low, weights["contract"], slope, weights["expand"]
    )
    grad_mixed = weight_grad("expand", mixed_rows, grad_upper, grad_mixed)
    normal_two, factor_two = row_stats(hidden)
    gain_two_grad = jnp.sum(grad_mixed * normal_two, axis=0)
    shift_two_grad = jnp.sum(grad_mixed, axis=0)
    grad_hidden = grad_full + norm_back(grad_mixed * weights["gain_two"], normal_two, factor_two)
    grad_attended = grad_hidden.astype(LOW)
    grad_context = matmul_right(grad_attended, weights["output"]).astype(LOW)
    grad_context = weight_grad("output", context, grad_attended, grad_context)
    grad_queries, grad_keys, grad_values = attend_backward(
        clips, length, queries, key_rows, value_rows, lse, grad_context
    )
    grad_proj = jnp.concatenate([grad_queries, grad_keys, grad_values], 1)
    grad_proj = weight_grad("project", normed, grad_proj, grad_proj)
    grad_normed = matmul_right(grad_proj, weights["project"])
    normal_one, factor_one = row_stats(rows_in.astype(FULL))
    gain_one_grad = jnp.sum(grad_normed * normal_one, axis=0)
    shift_one_grad = jnp.sum(grad_normed, axis=0)
    grad_in = grad_hidden + norm_back(grad_normed * weights["gain_one"], normal_one, factor_one)

    def total(part):
        return jnp.sum(part.astype(FULL), axis=0)

    small = dict(
        gain_one=gain_one_grad,
        shift_one=shift_one_grad,
        bias_query=total(grad_queries),
        bias_value=total(grad_values),
        bias_output=total(grad_attended),
        gain_two=gain_two_grad,
        shift_two=shift_two_grad,
        bias_expand=bias_expand_grad[0],
        bias_contract=total(grad_low),
    )
    return grad_in.astype(LOW), small


SMALL = (
    "gain_one",
    "shift_one",
    "bias_query",
    "bias_value",
    "bias_output",
    "gain_two",
    "shift_two",
    "bias_contract",
    "bias_expand",
)
LARGE = ("project", "output", "expand", "contract")
ORDER = (
    "gain_one",
    "shift_one",
    "project",
    "bias_query",
    "bias_value",
    "output",
    "bias_output",
    "gain_two",
    "shift_two",
    "expand",
    "bias_expand",
    "contract",
    "bias_contract",
)


def partner(axis, bit):
    return [(i, i ^ bit) for i in range(lax.axis_size(axis))]


def swap(block, axis, bit):
    return lax.ppermute(block, axis, partner(axis, bit))


def pick(stack, index, axis):
    return lax.dynamic_index_in_dim(stack, index, axis, keepdims=False)


def small_mesh():
    return lax.axis_size("fsdp") == 4 and lax.axis_size("rep") == 4


def order_kernel(place_ref, here_ref, there_ref, whole_ref, sems):
    rows = here_ref.shape[0] // 2
    half = rows // 2
    copies = []
    for source, ref in enumerate((here_ref, there_ref)):
        for piece, (start, size) in enumerate(((0, rows), (rows, half), (rows + half, half))):
            target = pl.multiple_of(place_ref[source, piece], 16)
            copies.append(
                pltpu.make_async_copy(
                    ref.at[pl.ds(start, size)],
                    whole_ref.at[pl.ds(target, size)],
                    sems.at[source, piece],
                )
            )
    for copy in copies:
        copy.start()
    for copy in copies:
        copy.wait()


def in_order(places, here, there):
    return pl.pallas_call(
        order_kernel,
        in_specs=[
            pl.BlockSpec(memory_space=pltpu.SMEM),
            pl.BlockSpec(memory_space=pl.ANY),
            pl.BlockSpec(memory_space=pl.ANY),
        ],
        out_specs=pl.BlockSpec(memory_space=pltpu.VMEM),
        out_shape=jax.ShapeDtypeStruct((2 * here.shape[0], here.shape[1]), here.dtype),
        scratch_shapes=[pltpu.SemaphoreType.DMA((2, 3))],
        compiler_params=pltpu.CompilerParams(vmem_limit_bytes=32 * 1024 * 1024),
        cost_estimate=BRIEF,
        name="shards_in_order",
    )(places, here, there)


class GatherChain:
    def __init__(self, shard, halves):
        self.shard = shard
        self.halves = halves
        if not small_mesh():
            self.mine = lax.all_gather(shard, "fsdp", axis=0, tiled=True)
            return
        rows, columns = shard.shape
        self.side = lax.axis_index("rep") % 2 if halves else jnp.int32(0)
        sent = pick(shard.reshape(2, rows // 2, columns), self.side, 0) if halves else shard
        self.mine = swap(sent, "fsdp", 2)

    def arrive(self, token):
        self.mine, token = lax.optimization_barrier((self.mine, token))
        return token

    def pass_on(self):
        if small_mesh() and self.halves:
            self.other = swap(self.mine, "rep", 1)

    def finish(self):
        if not small_mesh():
            return self.mine
        rows = self.shard.shape[0]
        half = rows // 2
        spot = lax.axis_index("fsdp")
        pieces = [self.shard, self.mine] + ([self.other] if self.halves else [])
        here = jnp.concatenate(pieces, 0)
        there = swap(here, "fsdp", 1)
        places = jnp.stack(
            [
                jnp.stack(
                    [base * rows, (base ^ 2) * rows + self.side * half, (base ^ 2) * rows + (1 - self.side) * half]
                )
                for base in (spot, spot ^ 1)
            ]
        ).astype(jnp.int32)
        return in_order(places, here, there)


def gather_small(packed):
    if not small_mesh():
        return lax.all_gather(packed, "fsdp", axis=0, tiled=True)
    spot = lax.axis_index("fsdp")
    far = swap(packed, "fsdp", 2)
    low = spot < 2
    here = jnp.stack([jnp.where(low, packed, far), jnp.where(low, far, packed)])
    there = swap(here, "fsdp", 1)
    even = spot % 2 == 0
    spread = jnp.concatenate([jnp.where(even, here, there), jnp.where(even, there, here)], 1)
    return spread.reshape(4, packed.shape[1])


def gather_vectors(vectors):
    packed = jnp.concatenate([vectors[name] for name in SMALL], 1)
    spread = gather_small(packed)
    devices = spread.shape[0]
    size = vectors["gain_one"].shape[1]
    count = len(SMALL) - 1
    rows = spread[:, : count * size].reshape(devices, count, size).transpose(1, 0, 2)
    rows = rows.reshape(count, devices * size).astype(FULL)
    weights = {name: rows[i] for i, name in enumerate(SMALL[:-1])}
    weights[SMALL[-1]] = spread[:, count * size :].reshape(-1).astype(FULL)
    return weights


def plus(left, right):
    return (left.astype(FULL) + right.astype(FULL)).astype(LOW)


class ReduceChain:
    def __init__(self, grad):
        self.grad = grad
        self.step = 0
        if not small_mesh():
            return
        self.spot = lax.axis_index("fsdp")
        self.side = lax.axis_index("rep") % 2
        split = grad.reshape((2, 2) + grad.shape[1:])
        self.keep = pick(split, self.spot % 2, 1)
        self.come = swap(pick(split, 1 - self.spot % 2, 1), "fsdp", 1)

    def advance(self, token):
        if not small_mesh():
            return token
        come, token = lax.optimization_barrier((self.come, token))
        self.step += 1
        if self.step == 5:
            even = self.side == 0
            low = jnp.where(even, self.keep, come)
            high = jnp.where(even, come, self.keep)
            self.owned = jnp.concatenate([low, high], 0).astype(FULL)
            return token
        total = plus(self.keep, come)
        if self.step == 1:
            self.keep = pick(total, self.spot // 2, 0)
            self.come = swap(pick(total, 1 - self.spot // 2, 0), "fsdp", 2)
        elif self.step == 2:
            halves = total.reshape(2, total.shape[0] // 2, total.shape[1])
            self.keep = pick(halves, self.side, 0)
            self.come = swap(pick(halves, 1 - self.side, 0), "rep", 1)
        elif self.step == 3:
            self.keep = total
            self.come = swap(total, "rep", 2)
        else:
            self.keep = total
            self.come = swap(total, "rep", 1)
        return tie(token, total)

    def finish(self):
        if not small_mesh():
            owned = lax.psum_scatter(self.grad, "fsdp", scatter_dimension=0, tiled=True)[0]
            return lax.psum(owned, "rep").astype(FULL)
        return self.owned


def pack_vectors(small, devices, width):
    parts = [small[name].reshape(devices, -1) for name in SMALL]
    packed = jnp.concatenate(parts, 1)
    rows = -(-packed.shape[1] // (32 * width)) * 32
    packed = jnp.pad(packed, ((0, 0), (0, rows * width - packed.shape[1])))
    return packed.reshape(devices, rows, width).astype(LOW)


def unpack_vectors(rows, vectors):
    flat = rows.reshape(-1)
    place = 0
    owned = {}
    for name in SMALL:
        size = vectors[name].shape[1]
        owned[name] = flat[place : place + size]
        place += size
    return owned


def local(inputs, cotangent, live_slots, *params):
    vectors = {name: part for name, part in zip(ORDER, params) if name in SMALL}
    shards = {name: part[0] for name, part in zip(ORDER, params) if name in LARGE}
    micro_count, clips, length, width = inputs.shape
    rows = clips * length
    first = lax.axis_index("section") == 0
    inputs = inputs.reshape(micro_count, rows, width)
    live = jnp.repeat(live_slots.reshape(micro_count, clips, 1), length, axis=1)
    cotangent = cotangent.reshape(micro_count, rows, width) * (live == 1).astype(LOW)
    gathers = {name: GatherChain(shards[name], name in ("project", "expand")) for name in LARGE}
    weights = gather_vectors(vectors)

    def forward(rows_in):
        return layer_forward(weights, clips, length, rows_in)

    def onward(rows_out):
        return lax.ppermute(rows_out, "section", [(0, 1)])

    def back(grad_rows):
        return lax.ppermute(grad_rows, "section", [(1, 0)])

    def begin(normed):
        chain = gathers["project"]
        normed = chain.arrive(normed)
        chain.pass_on()
        weights["project"] = chain.finish()
        return normed

    def before(queries):
        chain = gathers["expand"]
        queries = chain.arrive(queries)
        chain.pass_on()
        return queries

    def after(context):
        for name in ("output", "expand"):
            chain = gathers[name]
            context = chain.arrive(context)
            weights[name] = chain.finish()
        return context

    def last(active):
        chain = gathers["contract"]
        active = chain.arrive(active)
        weights["contract"] = chain.finish()
        return active

    out_a, _ = layer_forward(weights, clips, length, inputs[0], begin, before, after, last)
    out_b, kept_odd = forward(jnp.where(first, inputs[1], onward(out_a)))

    def backward(kept, grad_low, weight_grad):
        return layer_backward(weights, clips, length, kept, grad_low, weight_grad)

    factors = {}
    chains = {}
    grads = {}

    devices = lax.axis_size("fsdp")

    def no_grad(name, left, right, onto):
        return onto

    def first_grad(name, left, right, onto):
        factors[name] = (left, right)
        return onto

    def start_chains(name, grad):
        split = grad.reshape(devices, grad.shape[0] // devices, grad.shape[1])
        count = 1 if name == "output" else 2
        part = split.shape[1] // count
        for piece in range(count):
            chains[name, piece] = ReduceChain(split[:, piece * part : (piece + 1) * part])

    def last_grad(name, left, right, onto):
        onto = advance(onto, ahead[name])
        old_left, old_right = factors[name]
        left = jnp.concatenate([old_left, left], 0)
        right = jnp.concatenate([old_right, right], 0)
        if name == "output":
            grads[name] = matmul_left(left, right).astype(LOW)
        else:
            grad = matmul_left(left, tie(right, onto)).astype(LOW)
            start_chains(name, grad)
            onto = tie(onto, grad)
        return advance(onto, behind[name])

    con, exp, pro, out = "contract", "expand", "project", "output"
    p0, p1, e0, e1, c0, c1, o0 = (pro, 0), (pro, 1), (exp, 0), (exp, 1), (con, 0), (con, 1), (out, 0)
    ahead = {con: (), exp: (c0,), out: (), pro: (e0, c0, c1)}
    behind = {con: (c0, c1), exp: (c0,), out: (e0, e1, c1, c1), pro: (p0, p1, e1)}

    def advance(token, dues):
        for due in dues:
            token = chains[due].advance(token)
        return token

    received = onward(out_b)
    grad_a, _ = backward(kept_odd, cotangent[0], no_grad)
    returned = back(grad_a)
    out_c, kept_even = forward(tie(jnp.where(first, inputs[0], received), grad_a))
    section_outputs = jnp.stack([jnp.where(first, out_c, out_b), jnp.where(first, out_b, out_c)])

    grad_b, small_b = backward(kept_even, jnp.where(first, returned, cotangent[1]), first_grad)
    returned = back(grad_b)
    section_outputs, returned = lax.optimization_barrier((section_outputs, returned))
    grad_c, small_c = backward(kept_odd, jnp.where(first, returned, cotangent[0]), last_grad)

    small = {name: small_b[name] + small_c[name] for name in SMALL}
    extra = pack_vectors(small, devices, width)
    last = grads["output"].reshape(devices, -1, width)
    chains["output", 0] = ReduceChain(jnp.concatenate([last, extra], 1))
    grad_c = advance(
        grad_c,
        (o0, e0, e1, c0, c1, p0, e0, p1, p0, e1, e0, p1, o0, p0, o0, e1, p1, p0, o0, p1, o0),
    )
    section_input_grads = jnp.stack([jnp.where(first, grad_b, grad_c), jnp.where(first, grad_c, grad_b)])
    owned = {
        name: jnp.concatenate([chains[name, piece].finish() for piece in range(2)], 0)
        for name in (con, exp, pro)
    }
    tail = chains[out, 0].finish()
    count = last.shape[1]
    owned[out] = tail[:count]
    owned.update(unpack_vectors(tail[count:], vectors))
    shape_out = (1, micro_count, clips, length, width)
    return (
        section_outputs.reshape(shape_out),
        section_input_grads.reshape(shape_out),
    ) + tuple(owned[name][None] for name in ORDER)


def solution(mesh):
    rows_spec = P(None, ("fsdp", "rep"), None, None)
    vector = P("section", "fsdp")
    matrix = P("section", "fsdp", None)
    params = tuple(matrix if name in LARGE else vector for name in ORDER)
    in_specs = (rows_spec, rows_spec, P(None, ("fsdp", "rep"))) + params
    out_rows = P("section", None, ("fsdp", "rep"), None, None)
    out_specs = (out_rows, out_rows) + params
    return jax.shard_map(local, mesh=mesh, in_specs=in_specs, out_specs=out_specs, check_vma=False)
```

```python
import math

import jax
import jax.numpy as jnp
from jax import lax
from jax.experimental import pallas as pl
from jax.experimental.pallas import tpu as pltpu
from jax.sharding import PartitionSpec as P

HEADS = 12
HD = 64
PAIR = 2 * HD
SCALE = HD ** (-0.5)
epsilon = 1e-05
LOW = jnp.bfloat16
FULL = jnp.float32
BRIEF = pl.CostEstimate(flops=1024, bytes_accessed=1024, transcendentals=0)


def matmul(left, right):
    return jnp.dot(left, right, preferred_element_type=FULL)


def matmul_left(left, right):
    return lax.dot_general(left, right, (((0,), (0,)), ((), ())), preferred_element_type=FULL)


def matmul_right(left, right):
    return lax.dot_general(left, right, (((1,), (1,)), ((), ())), preferred_element_type=FULL)


def row_stats(values_in):
    mean_row = jnp.mean(values_in, axis=-1, keepdims=True)
    centered = values_in - mean_row
    factor = lax.rsqrt(jnp.mean(centered * centered, axis=-1, keepdims=True) + epsilon)
    return (centered * factor, factor)


def norm_back(grad_norm, normal, factor):
    first_mean = jnp.mean(grad_norm, axis=-1, keepdims=True)
    second_mean = jnp.mean(grad_norm * normal, axis=-1, keepdims=True)
    return factor * (grad_norm - first_mean - normal * second_mean)


def head_mask(head):
    lanes = lax.broadcasted_iota(jnp.int32, (1, PAIR), 1)
    return (lanes >= head * HD) & (lanes < (head + 1) * HD)


def only_head(rows, head):
    return jnp.where(head_mask(head), rows, jnp.zeros_like(rows))


def attend_kernel(q_ref, k_ref, v_ref, context_ref, lse_ref):
    queries = q_ref[...]
    keys = k_ref[...] * jnp.asarray(SCALE, LOW)
    values_t = v_ref[...].T
    pieces = []
    for head in range(2):
        scores = matmul_right(only_head(keys, head), queries)
        top = jnp.max(scores, axis=0, keepdims=True)
        exponent = jnp.exp(scores - top)
        total = jnp.sum(exponent, axis=0, keepdims=True)
        lse_ref[0, head : head + 1, :] = top + jnp.log(total)
        part = matmul(values_t[head * HD : (head + 1) * HD], exponent.astype(LOW))
        pieces.append(part * (1.0 / total))
    context_ref[...] = jnp.concatenate(pieces, 0).T.astype(LOW)


def attend_back_kernel(q_ref, k_ref, v_ref, lse_ref, g_ref, dq_ref, dk_ref, dv_ref):
    scale = jnp.asarray(SCALE, LOW)
    queries = q_ref[...]
    keys = k_ref[...] * scale
    values = v_ref[...]
    grads = g_ref[...]
    scaled_queries = queries * scale
    keys_t = keys.T
    pieces = []
    key_grad = None
    value_grad = None
    for head in range(2):
        grad_head = only_head(grads, head)
        scores = matmul_right(only_head(keys, head), queries)
        probs = jnp.exp(scores - lse_ref[0, head : head + 1, :])
        grad_probs = matmul_right(values, grad_head)
        value_part = matmul(probs.astype(LOW), grad_head)
        inner = jnp.sum(probs * grad_probs, axis=0, keepdims=True)
        grad_scores = (probs * (grad_probs - inner)).astype(LOW)
        key_part = matmul(grad_scores, only_head(scaled_queries, head))
        pieces.append(matmul(keys_t[head * HD : (head + 1) * HD], grad_scores))
        key_grad = key_part if key_grad is None else key_grad + key_part
        value_grad = value_part if value_grad is None else value_grad + value_part
    dq_ref[...] = jnp.concatenate(pieces, 0).T.astype(LOW)
    dk_ref[...] = key_grad.astype(LOW)
    dv_ref[...] = value_grad.astype(LOW)


def ffn_up_kernel(mixed_ref, expand_ref, bias_ref, active_ref, slope_ref):
    rows = mixed_ref.shape[0]
    part = rows // 4
    bias = bias_ref[...]
    for piece in range(4):
        span = pl.ds(piece * part, part)
        upper = matmul(mixed_ref[span, :], expand_ref[...]) + bias
        active, slope = gelu_parts(upper)
        active_ref[span, :] = active.astype(LOW)
        slope_ref[span, :] = slope.astype(LOW)


def ffn_up(mixed_rows, expand, bias):
    rows, width = mixed_rows.shape
    hidden_units = expand.shape[1]
    step = 512
    block = pl.BlockSpec((rows, step), lambda j: (0, j))
    return pl.pallas_call(
        ffn_up_kernel,
        grid=(hidden_units // step,),
        in_specs=[
            pl.BlockSpec((rows, width), lambda j: (0, 0)),
            pl.BlockSpec((width, step), lambda j: (0, j)),
            pl.BlockSpec((1, step), lambda j: (0, j)),
        ],
        out_specs=[block, block],
        out_shape=[jax.ShapeDtypeStruct((rows, hidden_units), LOW)] * 2,
        compiler_params=pltpu.CompilerParams(vmem_limit_bytes=40 * 1024 * 1024),
        cost_estimate=BRIEF,
        name="ffn_up",
    )(mixed_rows, expand, bias.reshape(1, hidden_units))


def ffn_whole_kernel(
    mixed_ref, expand_ref, bias_ref, contract_ref, hidden_ref, out_bias_ref, active_ref, slope_ref, result_ref, total_ref
):
    step = pl.program_id(0)

    @pl.when(step == 0)
    def _():
        total_ref[...] = hidden_ref[...] + out_bias_ref[...]

    rows = mixed_ref.shape[0]
    part = rows // 4
    bias = bias_ref[...]
    for piece in range(4):
        span = pl.ds(piece * part, part)
        upper = matmul(mixed_ref[span, :], expand_ref[...]) + bias
        active, slope = gelu_parts(upper)
        active = active.astype(LOW)
        active_ref[span, :] = active
        slope_ref[span, :] = slope.astype(LOW)
        total_ref[span, :] += matmul(active, contract_ref[...])

    @pl.when(step == pl.num_programs(0) - 1)
    def _():
        result_ref[...] = total_ref[...].astype(LOW)


def ffn_whole(mixed_rows, expand, bias, contract, hidden, out_bias):
    rows, width = mixed_rows.shape
    hidden_units = expand.shape[1]
    step = 512
    block = pl.BlockSpec((rows, step), lambda j: (0, j))
    whole = pl.BlockSpec((rows, width), lambda j: (0, 0))
    return pl.pallas_call(
        ffn_whole_kernel,
        grid=(hidden_units // step,),
        in_specs=[
            whole,
            pl.BlockSpec((width, step), lambda j: (0, j)),
            pl.BlockSpec((1, step), lambda j: (0, j)),
            pl.BlockSpec((step, width), lambda j: (j, 0)),
            whole,
            pl.BlockSpec((1, width), lambda j: (0, 0)),
        ],
        out_specs=[block, block, whole],
        out_shape=[
            jax.ShapeDtypeStruct((rows, hidden_units), LOW),
            jax.ShapeDtypeStruct((rows, hidden_units), LOW),
            jax.ShapeDtypeStruct((rows, width), LOW),
        ],
        scratch_shapes=[pltpu.VMEM((rows, width), FULL)],
        compiler_params=pltpu.CompilerParams(vmem_limit_bytes=44 * 1024 * 1024),
        cost_estimate=BRIEF,
        name="ffn_whole",
    )(mixed_rows, expand, bias.reshape(1, hidden_units), contract, hidden, out_bias.reshape(1, width))


def ffn_back_kernel(grad_ref, contract_ref, slope_ref, expand_ref, upper_ref, mixed_ref, sum_ref):
    @pl.when(pl.program_id(0) == 0)
    def _():
        mixed_ref[...] = jnp.zeros_like(mixed_ref)

    rows = grad_ref.shape[0]
    part = rows // 2
    total = None
    for piece in range(2):
        span = pl.ds(piece * part, part)
        grad_active = matmul_right(grad_ref[span, :], contract_ref[...])
        grad_upper = (grad_active * slope_ref[span, :].astype(FULL)).astype(LOW)
        upper_ref[span, :] = grad_upper
        column = jnp.sum(grad_upper.astype(FULL), axis=0, keepdims=True)
        total = column if total is None else total + column
        mixed_ref[span, :] += matmul_right(grad_upper, expand_ref[...])
    sum_ref[...] = total


def ffn_back(grad_low, contract, slope, expand):
    rows, width = grad_low.shape
    hidden_units = contract.shape[0]
    step = 512
    block = pl.BlockSpec((rows, step), lambda j: (0, j))
    whole = pl.BlockSpec((rows, width), lambda j: (0, 0))
    return pl.pallas_call(
        ffn_back_kernel,
        grid=(hidden_units // step,),
        in_specs=[
            whole,
            pl.BlockSpec((step, width), lambda j: (j, 0)),
            block,
            pl.BlockSpec((width, step), lambda j: (0, j)),
        ],
        out_specs=[block, whole, pl.BlockSpec((1, step), lambda j: (0, j))],
        out_shape=[
            jax.ShapeDtypeStruct((rows, hidden_units), LOW),
            jax.ShapeDtypeStruct((rows, width), FULL),
            jax.ShapeDtypeStruct((1, hidden_units), FULL),
        ],
        compiler_params=pltpu.CompilerParams(vmem_limit_bytes=40 * 1024 * 1024),
        cost_estimate=BRIEF,
        name="ffn_back",
    )(grad_low, contract, slope, expand)


def attend_forward(clips, length, queries, key_rows, value_rows):
    rows, width = queries.shape
    pairs = width // PAIR
    block = pl.BlockSpec((length, PAIR), lambda c, j: (c, j))
    lse_block = pl.BlockSpec((1, 8, length), lambda c, j: (c * pairs + j, 0, 0))
    return pl.pallas_call(
        attend_kernel,
        grid=(clips, pairs),
        in_specs=[block] * 3,
        out_specs=[block, lse_block],
        out_shape=[
            jax.ShapeDtypeStruct((rows, width), LOW),
            jax.ShapeDtypeStruct((clips * pairs, 8, length), FULL),
        ],
        compiler_params=pltpu.CompilerParams(vmem_limit_bytes=40 * 1024 * 1024),
        cost_estimate=BRIEF,
        name="attend_forward",
    )(queries, key_rows, value_rows)


def attend_backward(clips, length, queries, key_rows, value_rows, lse, grad_context, low=0, high=None):
    rows, width = queries.shape
    pairs = width // PAIR
    high = pairs if high is None else high
    block = pl.BlockSpec((length, PAIR), lambda c, j: (c, low + j))
    lse_block = pl.BlockSpec((1, 8, length), lambda c, j: (c * pairs + low + j, 0, 0))
    out_block = pl.BlockSpec((length, PAIR), lambda c, j: (c, j))
    return pl.pallas_call(
        attend_back_kernel,
        grid=(clips, high - low),
        in_specs=[block] * 3 + [lse_block, block],
        out_specs=[out_block] * 3,
        out_shape=[jax.ShapeDtypeStruct((rows, (high - low) * PAIR), LOW)] * 3,
        compiler_params=pltpu.CompilerParams(vmem_limit_bytes=48 * 1024 * 1024),
        cost_estimate=BRIEF,
        name="attend_backward",
    )(queries, key_rows, value_rows, lse, grad_context)


def gelu_parts(upper):
    size = jnp.abs(upper)
    turn = 1.0 / (1.0 + (0.3275911 / math.sqrt(2.0)) * size)
    bell = jnp.exp(-0.5 * upper * upper)
    series = turn * (
        0.5 * 0.254829592
        + turn
        * (
            0.5 * -0.284496736
            + turn * (0.5 * 1.421413741 + turn * (0.5 * -1.453152027 + turn * (0.5 * 1.061405429)))
        )
    )
    tail = series * bell
    below = jnp.where(upper < 0, tail, 1.0 - tail)
    return upper * below, below + upper * bell * (1.0 / math.sqrt(2.0 * math.pi))


def layer_forward(weights, clips, length, rows_in, begin=None, before=None, after=None, last=None):
    width = rows_in.shape[1]
    token_rows = rows_in.astype(FULL)
    normal_one, _ = row_stats(token_rows)
    normed = (normal_one * weights["gain_one"] + weights["shift_one"]).astype(LOW)
    if begin is not None:
        normed = begin(normed)
    projected = matmul(normed, weights["project"])
    queries = (projected[:, :width] + weights["bias_query"]).astype(LOW)
    key_rows = projected[:, width : 2 * width].astype(LOW)
    value_rows = (projected[:, 2 * width :] + weights["bias_value"]).astype(LOW)
    if before is not None:
        queries = before(queries)
    context, lse = attend_forward(clips, length, queries, key_rows, value_rows)
    if after is not None:
        context = after(context)
    hidden = token_rows + (matmul(context, weights["output"]) + weights["bias_output"])
    normal_two, _ = row_stats(hidden)
    mixed_rows = (normal_two * weights["gain_two"] + weights["shift_two"]).astype(LOW)
    if last is not None:
        active, slope = ffn_up(mixed_rows, weights["expand"], weights["bias_expand"])
        active = last(active)
        result = (hidden + (matmul(active, weights["contract"]) + weights["bias_contract"])).astype(LOW)
    else:
        active, slope, result = ffn_whole(
            mixed_rows,
            weights["expand"],
            weights["bias_expand"],
            weights["contract"],
            hidden,
            weights["bias_contract"],
        )
    kept = (rows_in, normed, queries, key_rows, value_rows, lse, context, hidden, mixed_rows, active, slope)
    return result, kept


def tie(value, *others):
    return lax.optimization_barrier((value,) + others)[0]


def layer_backward(weights, clips, length, kept, grad_low, weight_grad):
    rows_in, normed, queries, key_rows, value_rows, lse, context, hidden, mixed_rows, active, slope = kept
    grad_full = grad_low.astype(FULL)
    grad_low = weight_grad("contract", active, grad_low, grad_low)
    grad_upper, grad_mixed, bias_expand_grad = ffn_back(
        grad_low, weights["contract"], slope, weights["expand"]
    )
    grad_mixed = weight_grad("expand", mixed_rows, grad_upper, grad_mixed)
    normal_two, factor_two = row_stats(hidden)
    gain_two_grad = jnp.sum(grad_mixed * normal_two, axis=0)
    shift_two_grad = jnp.sum(grad_mixed, axis=0)
    grad_hidden = grad_full + norm_back(grad_mixed * weights["gain_two"], normal_two, factor_two)
    grad_attended = grad_hidden.astype(LOW)
    grad_context = matmul_right(grad_attended, weights["output"]).astype(LOW)
    grad_context = weight_grad("output", context, grad_attended, grad_context)
    grad_queries, grad_keys, grad_values = attend_backward(
        clips, length, queries, key_rows, value_rows, lse, grad_context
    )
    grad_proj = jnp.concatenate([grad_queries, grad_keys, grad_values], 1)
    grad_proj = weight_grad("project", normed, grad_proj, grad_proj)
    grad_normed = matmul_right(grad_proj, weights["project"])
    normal_one, factor_one = row_stats(rows_in.astype(FULL))
    gain_one_grad = jnp.sum(grad_normed * normal_one, axis=0)
    shift_one_grad = jnp.sum(grad_normed, axis=0)
    grad_in = grad_hidden + norm_back(grad_normed * weights["gain_one"], normal_one, factor_one)

    def total(part):
        return jnp.sum(part.astype(FULL), axis=0)

    small = dict(
        gain_one=gain_one_grad,
        shift_one=shift_one_grad,
        bias_query=total(grad_queries),
        bias_value=total(grad_values),
        bias_output=total(grad_attended),
        gain_two=gain_two_grad,
        shift_two=shift_two_grad,
        bias_expand=bias_expand_grad[0],
        bias_contract=total(grad_low),
    )
    return grad_in.astype(LOW), small


SMALL = (
    "gain_one",
    "shift_one",
    "bias_query",
    "bias_value",
    "bias_output",
    "gain_two",
    "shift_two",
    "bias_contract",
    "bias_expand",
)
LARGE = ("project", "output", "expand", "contract")
ORDER = (
    "gain_one",
    "shift_one",
    "project",
    "bias_query",
    "bias_value",
    "output",
    "bias_output",
    "gain_two",
    "shift_two",
    "expand",
    "bias_expand",
    "contract",
    "bias_contract",
)


def partner(axis, bit):
    return [(i, i ^ bit) for i in range(lax.axis_size(axis))]


def swap(block, axis, bit):
    return lax.ppermute(block, axis, partner(axis, bit))


def pick(stack, index, axis):
    return lax.dynamic_index_in_dim(stack, index, axis, keepdims=False)


def small_mesh():
    return lax.axis_size("fsdp") == 4 and lax.axis_size("rep") == 4


def order_kernel(place_ref, here_ref, there_ref, whole_ref, sems):
    rows = here_ref.shape[0] // 2
    half = rows // 2
    copies = []
    for source, ref in enumerate((here_ref, there_ref)):
        for piece, (start, size) in enumerate(((0, rows), (rows, half), (rows + half, half))):
            target = pl.multiple_of(place_ref[source, piece], 16)
            copies.append(
                pltpu.make_async_copy(
                    ref.at[pl.ds(start, size)],
                    whole_ref.at[pl.ds(target, size)],
                    sems.at[source, piece],
                )
            )
    for copy in copies:
        copy.start()
    for copy in copies:
        copy.wait()


def in_order(places, here, there):
    return pl.pallas_call(
        order_kernel,
        in_specs=[
            pl.BlockSpec(memory_space=pltpu.SMEM),
            pl.BlockSpec(memory_space=pl.ANY),
            pl.BlockSpec(memory_space=pl.ANY),
        ],
        out_specs=pl.BlockSpec(memory_space=pltpu.VMEM),
        out_shape=jax.ShapeDtypeStruct((2 * here.shape[0], here.shape[1]), here.dtype),
        scratch_shapes=[pltpu.SemaphoreType.DMA((2, 3))],
        compiler_params=pltpu.CompilerParams(vmem_limit_bytes=32 * 1024 * 1024),
        cost_estimate=BRIEF,
        name="shards_in_order",
    )(places, here, there)


class GatherChain:
    def __init__(self, shard, halves):
        self.shard = shard
        self.halves = halves
        if not small_mesh():
            self.mine = lax.all_gather(shard, "fsdp", axis=0, tiled=True)
            return
        rows, columns = shard.shape
        self.side = lax.axis_index("rep") % 2 if halves else jnp.int32(0)
        sent = pick(shard.reshape(2, rows // 2, columns), self.side, 0) if halves else shard
        self.mine = swap(sent, "fsdp", 2)

    def arrive(self, token):
        self.mine, token = lax.optimization_barrier((self.mine, token))
        return token

    def pass_on(self):
        if small_mesh() and self.halves:
            self.other = swap(self.mine, "rep", 1)

    def finish(self):
        if not small_mesh():
            return self.mine
        rows = self.shard.shape[0]
        half = rows // 2
        spot = lax.axis_index("fsdp")
        pieces = [self.shard, self.mine] + ([self.other] if self.halves else [])
        here = jnp.concatenate(pieces, 0)
        there = swap(here, "fsdp", 1)
        places = jnp.stack(
            [
                jnp.stack(
                    [base * rows, (base ^ 2) * rows + self.side * half, (base ^ 2) * rows + (1 - self.side) * half]
                )
                for base in (spot, spot ^ 1)
            ]
        ).astype(jnp.int32)
        return in_order(places, here, there)


def gather_small(packed):
    if not small_mesh():
        return lax.all_gather(packed, "fsdp", axis=0, tiled=True)
    spot = lax.axis_index("fsdp")
    far = swap(packed, "fsdp", 2)
    low = spot < 2
    here = jnp.stack([jnp.where(low, packed, far), jnp.where(low, far, packed)])
    there = swap(here, "fsdp", 1)
    even = spot % 2 == 0
    spread = jnp.concatenate([jnp.where(even, here, there), jnp.where(even, there, here)], 1)
    return spread.reshape(4, packed.shape[1])


def gather_vectors(vectors):
    packed = jnp.concatenate([vectors[name] for name in SMALL], 1)
    spread = gather_small(packed)
    devices = spread.shape[0]
    size = vectors["gain_one"].shape[1]
    count = len(SMALL) - 1
    rows = spread[:, : count * size].reshape(devices, count, size).transpose(1, 0, 2)
    rows = rows.reshape(count, devices * size).astype(FULL)
    weights = {name: rows[i] for i, name in enumerate(SMALL[:-1])}
    weights[SMALL[-1]] = spread[:, count * size :].reshape(-1).astype(FULL)
    return weights


def plus(left, right):
    return (left.astype(FULL) + right.astype(FULL)).astype(LOW)


class ReduceChain:
    def __init__(self, grad):
        self.grad = grad
        self.step = 0
        if not small_mesh():
            return
        self.spot = lax.axis_index("fsdp")
        self.side = lax.axis_index("rep") % 2
        split = grad.reshape((2, 2) + grad.shape[1:])
        self.keep = pick(split, self.spot % 2, 1)
        self.come = swap(pick(split, 1 - self.spot % 2, 1), "fsdp", 1)

    def advance(self, token):
        if not small_mesh():
            return token
        come, token = lax.optimization_barrier((self.come, token))
        self.step += 1
        if self.step == 5:
            even = self.side == 0
            low = jnp.where(even, self.keep, come)
            high = jnp.where(even, come, self.keep)
            self.owned = jnp.concatenate([low, high], 0).astype(FULL)
            return token
        total = plus(self.keep, come)
        if self.step == 1:
            self.keep = pick(total, self.spot // 2, 0)
            self.come = swap(pick(total, 1 - self.spot // 2, 0), "fsdp", 2)
        elif self.step == 2:
            halves = total.reshape(2, total.shape[0] // 2, total.shape[1])
            self.keep = pick(halves, self.side, 0)
            self.come = swap(pick(halves, 1 - self.side, 0), "rep", 1)
        elif self.step == 3:
            self.keep = total
            self.come = swap(total, "rep", 2)
        else:
            self.keep = total
            self.come = swap(total, "rep", 1)
        return tie(token, total)

    def finish(self):
        if not small_mesh():
            owned = lax.psum_scatter(self.grad, "fsdp", scatter_dimension=0, tiled=True)[0]
            return lax.psum(owned, "rep").astype(FULL)
        return self.owned


def pack_vectors(small, devices, width):
    parts = [small[name].reshape(devices, -1) for name in SMALL]
    packed = jnp.concatenate(parts, 1)
    rows = -(-packed.shape[1] // (32 * width)) * 32
    packed = jnp.pad(packed, ((0, 0), (0, rows * width - packed.shape[1])))
    return packed.reshape(devices, rows, width).astype(LOW)


def unpack_vectors(rows, vectors):
    flat = rows.reshape(-1)
    place = 0
    owned = {}
    for name in SMALL:
        size = vectors[name].shape[1]
        owned[name] = flat[place : place + size]
        place += size
    return owned


def local(inputs, cotangent, live_slots, *params):
    vectors = {name: part for name, part in zip(ORDER, params) if name in SMALL}
    shards = {name: part[0] for name, part in zip(ORDER, params) if name in LARGE}
    micro_count, clips, length, width = inputs.shape
    rows = clips * length
    first = lax.axis_index("section") == 0
    inputs = inputs.reshape(micro_count, rows, width)
    live = jnp.repeat(live_slots.reshape(micro_count, clips, 1), length, axis=1)
    cotangent = cotangent.reshape(micro_count, rows, width) * (live == 1).astype(LOW)
    gathers = {name: GatherChain(shards[name], name in ("project", "expand")) for name in LARGE}
    weights = gather_vectors(vectors)

    def forward(rows_in):
        return layer_forward(weights, clips, length, rows_in)

    def onward(rows_out):
        return lax.ppermute(rows_out, "section", [(0, 1)])

    def back(grad_rows):
        return lax.ppermute(grad_rows, "section", [(1, 0)])

    def begin(normed):
        chain = gathers["project"]
        normed = chain.arrive(normed)
        chain.pass_on()
        weights["project"] = chain.finish()
        return normed

    def before(queries):
        chain = gathers["expand"]
        queries = chain.arrive(queries)
        chain.pass_on()
        return queries

    def after(context):
        for name in ("output", "expand"):
            chain = gathers[name]
            context = chain.arrive(context)
            weights[name] = chain.finish()
        return context

    def last(active):
        chain = gathers["contract"]
        active = chain.arrive(active)
        weights["contract"] = chain.finish()
        return active

    out_a, _ = layer_forward(weights, clips, length, inputs[0], begin, before, after, last)
    out_b, kept_odd = forward(jnp.where(first, inputs[1], onward(out_a)))

    def backward(kept, grad_low, weight_grad):
        return layer_backward(weights, clips, length, kept, grad_low, weight_grad)

    factors = {}
    chains = {}
    grads = {}

    devices = lax.axis_size("fsdp")

    def no_grad(name, left, right, onto):
        return onto

    def first_grad(name, left, right, onto):
        factors[name] = (left, right)
        return onto

    def start_chains(name, grad):
        split = grad.reshape(devices, grad.shape[0] // devices, grad.shape[1])
        count = 1 if name == "output" else 2
        part = split.shape[1] // count
        for piece in range(count):
            chains[name, piece] = ReduceChain(split[:, piece * part : (piece + 1) * part])

    def last_grad(name, left, right, onto):
        onto = advance(onto, ahead[name])
        old_left, old_right = factors[name]
        left = jnp.concatenate([old_left, left], 0)
        right = jnp.concatenate([old_right, right], 0)
        if name == "output":
            grads[name] = matmul_left(left, right).astype(LOW)
        else:
            grad = matmul_left(left, tie(right, onto)).astype(LOW)
            start_chains(name, grad)
            onto = tie(onto, grad)
        return advance(onto, behind[name])

    con, exp, pro, out = "contract", "expand", "project", "output"
    p0, p1, e0, e1, c0, c1, o0 = (pro, 0), (pro, 1), (exp, 0), (exp, 1), (con, 0), (con, 1), (out, 0)
    ahead = {con: (), exp: (c0,), out: (), pro: (e0, c0, c1)}
    behind = {con: (c0, c1), exp: (c0,), out: (e0, e1, c1, c1), pro: (p0, p1, e1)}

    def advance(token, dues):
        for due in dues:
            token = chains[due].advance(token)
        return token

    received = onward(out_b)
    grad_a, _ = backward(kept_odd, cotangent[0], no_grad)
    returned = back(grad_a)
    out_c, kept_even = forward(tie(jnp.where(first, inputs[0], received), grad_a))
    section_outputs = jnp.stack([jnp.where(first, out_c, out_b), jnp.where(first, out_b, out_c)])

    grad_b, small_b = backward(kept_even, jnp.where(first, returned, cotangent[1]), first_grad)
    returned = back(grad_b)
    section_outputs, returned = lax.optimization_barrier((section_outputs, returned))
    grad_c, small_c = backward(kept_odd, jnp.where(first, returned, cotangent[0]), last_grad)

    small = {name: small_b[name] + small_c[name] for name in SMALL}
    extra = pack_vectors(small, devices, width)
    last = grads["output"].reshape(devices, -1, width)
    chains["output", 0] = ReduceChain(jnp.concatenate([last, extra], 1))
    grad_c = advance(
        grad_c,
        (e0, p0, e1, c0, c1, p1, o0, e0, p0, e1, p1, e0, p0, o0, e1, p1, p0, o0, p1, o0, o0),
    )
    section_input_grads = jnp.stack([jnp.where(first, grad_b, grad_c), jnp.where(first, grad_c, grad_b)])
    owned = {
        name: jnp.concatenate([chains[name, piece].finish() for piece in range(2)], 0)
        for name in (con, exp, pro)
    }
    tail = chains[out, 0].finish()
    count = last.shape[1]
    owned[out] = tail[:count]
    owned.update(unpack_vectors(tail[count:], vectors))
    shape_out = (1, micro_count, clips, length, width)
    return (
        section_outputs.reshape(shape_out),
        section_input_grads.reshape(shape_out),
    ) + tuple(owned[name][None] for name in ORDER)


def solution(mesh):
    rows_spec = P(None, ("fsdp", "rep"), None, None)
    vector = P("section", "fsdp")
    matrix = P("section", "fsdp", None)
    params = tuple(matrix if name in LARGE else vector for name in ORDER)
    in_specs = (rows_spec, rows_spec, P(None, ("fsdp", "rep"))) + params
    out_rows = P("section", None, ("fsdp", "rep"), None, None)
    out_specs = (out_rows, out_rows) + params
    return jax.shard_map(local, mesh=mesh, in_specs=in_specs, out_specs=out_specs, check_vma=False)
```
